768 devices in a mesh: dp: 32 (over y, x_lo, core), mp: 24 (over z, x_hi).
Axes of the slice: x: 4 (x_hi: 2, x_lo: 2; x = x_hi * 2 + x_lo), y: 8, z: 12, core: 2. Of those that a mesh axis runs over, the one named last changes fastest.
Arguments:
- tokens: bfloat16 [1536, 8192], P(None, 'dp'), may hold values from -6 to 6
- gate_weight: bfloat16 [8192, 15360], P('dp', 'mp'), may hold values from -0.0625 to 0.0625
- up_weight: bfloat16 [8192, 15360], P('dp', 'mp'), may hold values from -0.0625 to 0.0625
- down_weight: bfloat16 [15360, 8192], P('mp', 'dp'), may hold values from -0.046875 to 0.046875
Outputs:
- mixed: bfloat16 [1536, 8192], P('mp', 'dp')
The draws below stay inside these ranges and needn't reach their ends.
All inputs are finite; a program needn't handle non-finite values.
Results may differ from the reference program's by a relative error of at most 0.0049.
Values may be sent and summed in bfloat16 or wider, within the bound.
A program may use at most 64 MiB of HBM per device.

```python
import jax
import jax.numpy as jnp

D = 8192
FF = 15360
ROWS = 1536


def block_levels(own_key, dims, pieces, least, largest):
    gain, own = 1.0, jax.random.fold_in(own_key, 6)
    for axis_at, shards_of in pieces:
        draws = jnp.exp(jax.random.uniform(jax.random.fold_in(own, axis_at), (shards_of,), jnp.float32, least / len(pieces), largest / len(pieces)))
        gain = gain * jnp.repeat(draws, dims[axis_at] // shards_of).reshape([-1 if axis == axis_at else 1 for axis in range(len(dims))])
    return gain


def normal_values(key, extent, spread, most, split=(), held_as=jnp.bfloat16):
    gain = block_levels(key, extent, split, -0.22, 0.18) if split else 1.0
    array = jax.random.normal(key, extent, jnp.float32) * spread * gain
    return jnp.minimum(jnp.maximum(array, -most), most).astype(held_as)


def setup_inputs(seed: int = 0) -> dict:
    arg_keys = jax.random.split(jax.random.key(seed), 5)
    return {
        "tokens": normal_values(arg_keys[0], (ROWS, D), 1.0, 6.0, ((1, 32),)),
        "gate_weight": normal_values(arg_keys[1], (D, FF), D ** -0.5, 0.0625, ((0, 32), (1, 24))),
        "up_weight": normal_values(arg_keys[2], (D, FF), D ** -0.5, 0.0625, ((0, 32), (1, 24))),
        "down_weight": normal_values(arg_keys[3], (FF, D), FF ** -0.5, 0.046875, ((0, 24), (1, 32))),
    }


def reference(tokens, gate_weight, up_weight, down_weight):
    gate = jnp.dot(tokens, gate_weight, preferred_element_type=jnp.float32)
    up = jnp.dot(tokens, up_weight, preferred_element_type=jnp.float32)
    hidden = (jax.nn.silu(gate) * up).astype(jnp.bfloat16)
    mixed = jnp.dot(hidden, down_weight, preferred_element_type=jnp.float32)
    return mixed.astype(jnp.bfloat16)
```

```python
import jax
import jax.numpy as jnp
from jax import lax
from jax.experimental import pallas as pl
from jax.experimental.pallas import tpu as pltpu
from jax.sharding import Mesh
from jax.sharding import PartitionSpec as P

AXES = ("y", "xl", "c", "z", "xh")
NY, NZ = 8, 12
DP = ("y", "xl", "c")
MP = ("z", "xh")
F = 640
MESH = pl.DeviceIdType.MESH
BF = jnp.bfloat16
F32 = jnp.float32


def dot(a, b):
    return jnp.dot(a, b, preferred_element_type=F32)


def hidden_kernel(
    tok, gw, uw, h_out,
    tok_b, w_b, part, s1s, s1r, s2s, s2r, s3s, s3r, s4s, s4r, xs, xr, hid,
    ex_s, ex_r, r1_s, r1_r, r2_s, r2_r, r3_s, r3_r, r4_s, r4_r, x_s, x_r,
    za_s, za_r, ya_s, ya_r, cf_s, cf_r,
):
    y, xl, c, z = (lax.axis_index(a) for a in AXES[:4])
    other_x, other_c = 1 - xl, 1 - c

    def at_y(d):
        return lax.rem(y + (d + NY), NY)

    def put(src, dst, ss, rs, **where):
        return pltpu.make_async_remote_copy(
            src_ref=src, dst_ref=dst, send_sem=ss, recv_sem=rs,
            device_id=where, device_id_type=MESH,
        )

    barrier = pltpu.get_barrier_semaphore()

    def greet(**where):
        pl.semaphore_signal(barrier, inc=1, device_id=where, device_id_type=MESH)

    greet(c=other_c)
    greet(xl=other_x)
    for d in range(1, NY):
        greet(y=at_y(d))
    for d in (1, -1):
        greet(y=at_y(d), xl=other_x)
    group = z // 3
    active = c == lax.rem(group, 2)
    from_x = group // 2
    my_first = 6 * xl + 3 * c
    for k in range(NZ):

        @pl.when(active & ((z != k) | (xl != from_x)))
        def _():
            greet(xl=from_x, z=k)

    mine = (z >= my_first) & (z < my_first + 3)
    pl.semaphore_wait(barrier, 2 + (NY - 1) + 2 + 6 - mine.astype(jnp.int32))

    exchange = [
        put(tok.at[pl.ds(6 * h + 3 * other_c, 3)], tok_b.at[h], ex_s.at[h], ex_r.at[h], c=other_c)
        for h in range(2)
    ] + [
        put(w, w_b.at[k], ex_s.at[2 + k], ex_r.at[2 + k], c=other_c)
        for k, w in enumerate((gw, uw))
    ]
    for cp in exchange:
        cp.start()
    for k, w in enumerate((gw, uw)):
        for h in range(2):
            a = tok[pl.ds(6 * h + 3 * c, 3)].reshape(384, 256)
            part[k, h] = dot(a, w[...]).reshape(3, NY, 16, F)
    for cp in exchange:
        cp.wait_recv()

    sent = list(exchange)

    def go(cp):
        cp.start()
        sent.append(cp)
        return cp

    def own(k, h, o):
        return part[k, h, :, o].reshape(48, F)

    far = at_y(4)
    for k in range(2):
        for h in range(2):
            a = tok_b[h, :, far].reshape(48, 256)
            s1s[k, h] = (own(k, h, far) + dot(a, w_b[k])).astype(BF)
    step1 = [
        go(put(s1s.at[k], s1r.at[k], r1_s.at[k], r1_r.at[k], y=at_y((-1, 1)[k]))) for k in range(2)
    ]
    for k in range(2):
        for h in range(2):
            a = tok_b[h].reshape(384, 256)
            part[k, h] = part[k, h] + dot(a, w_b[k]).reshape(3, NY, 16, F)

    step2 = [[None, None], [None, None]]

    def second(i, k):
        sign = (-1, 1)[i]
        for h in range(2):
            v = own(k, h, at_y(3 * sign))
            if i == k:
                v = v + s1r[k, h].astype(F32)
            s2s[i, k, h] = v.astype(BF)
        step2[i][k] = go(
            put(s2s.at[i, k], s2r.at[i, k], r2_s.at[i, k], r2_r.at[i, k], y=at_y(sign))
        )

    second(0, 1)
    second(1, 0)
    crossing = []
    for j in range(3):
        for k in range(2):
            xs[j, k] = own(k, other_x, at_y(j - 1)).astype(BF)
        crossing.append(go(put(xs.at[j], xr.at[j], x_s.at[j], x_r.at[j], xl=other_x)))
    for k in range(2):
        step1[k].wait_recv()
        second(k, k)

    step3 = {}
    for i, k in ((0, 1), (1, 0), (0, 0), (1, 1)):
        sign = (-1, 1)[i]
        step2[i][k].wait_recv()
        for h in range(2):
            s3s[i, k, h] = (own(k, h, at_y(2 * sign)) + s2r[i, k, h].astype(F32)).astype(BF)
        for t, where in ((0, xl), (1, other_x)):
            step3[i, k, t] = go(
                put(
                    s3s.at[i, k, where], s3r.at[i, k, t], r3_s.at[i, k, t], r3_r.at[i, k, t],
                    y=at_y(sign), xl=where,
                )
            )

    step4 = {}
    crossing[0].wait_recv()
    crossing[2].wait_recv()
    for i, k in ((0, 1), (1, 0), (0, 0), (1, 1)):
        sign = (-1, 1)[i]
        for t in range(2):
            step3[i, k, t].wait_recv()
        s4s[i, k] = (
            own(k, xl, at_y(sign))
            + s3r[i, k, 0].astype(F32)
            + s3r[i, k, 1].astype(F32)
            + xr[1 + sign, k].astype(F32)
        )
        step4[i, k] = go(
            put(s4s.at[i, k], s4r.at[i, k], r4_s.at[i, k], r4_r.at[i, k], y=at_y(sign))
        )
    crossing[1].wait_recv()
    total = []
    for k in range(2):
        for i in range(2):
            step4[i, k].wait_recv()
        total.append(own(k, xl, y) + s4r[0, k] + s4r[1, k] + xr[1, k].astype(F32))
    hid[...] = (jax.nn.silu(total[0]) * total[1]).astype(BF).reshape(3, 16, F)

    my_rows = h_out.at[pl.ds(pl.multiple_of(16 * y, 16), 16)]
    slot = my_rows.at[:, pl.ds(pl.multiple_of(z * F, 128), F)]
    for j in range(3):
        to_z = my_first + j
        same = put(hid.at[j], slot, za_s.at[j, 0], za_r, z=to_z)
        local = pltpu.make_async_copy(hid.at[j], slot, za_r)

        @pl.when(to_z != z)
        def _():
            same.start()

        @pl.when(to_z == z)
        def _():
            local.start()

        go(put(hid.at[j], slot, za_s.at[j, 1], za_r, z=to_z, xl=other_x))

    @pl.when(active)
    def _():
        pltpu.make_async_copy(my_rows, my_rows, za_r).wait()
        order = (1, 7, 2, 6, 3, 5, 4)
        outs = [put(my_rows, my_rows, ya_s.at[d], ya_r.at[d], y=at_y(d)) for d in order]
        for cp in outs:
            cp.start()
        first = put(my_rows, my_rows, cf_s.at[0], cf_r.at[0], c=other_c)
        first.start()
        forward = [first]
        for d, cp in zip(order, outs):
            rows = h_out.at[pl.ds(pl.multiple_of(16 * at_y(-d), 16), 16)]
            put(rows, rows, ya_s.at[d], ya_r.at[d], y=at_y(d)).wait_recv()
            f = put(rows, rows, cf_s.at[d], cf_r.at[d], c=other_c)
            f.start()
            forward.append(f)
        for cp in outs + forward:
            cp.wait_send()

    @pl.when(jnp.logical_not(active))
    def _():
        for d in range(NY):
            rows = h_out.at[pl.ds(pl.multiple_of(16 * at_y(-d), 16), 16)]
            put(rows, rows, cf_s.at[d], cf_r.at[d], c=other_c).wait_recv()

    for j in range(3):

        @pl.when(my_first + j != z)
        def _():
            put(hid.at[j], slot, za_s.at[j, 0], za_r, z=my_first + j).wait_send()

    for cp in sent:
        cp.wait_send()


def gathered_hidden(tokens, gate_weight, up_weight):
    dma = pltpu.SemaphoreType.DMA
    pair = [pltpu.VMEM((2, 2, 48, F), BF)] * 2
    twice = [pltpu.VMEM((2, 2, 2, 48, F), BF)] * 2
    return pl.pallas_call(
        hidden_kernel,
        out_shape=jax.ShapeDtypeStruct((16 * NY, NZ * F), BF),
        in_specs=[pl.BlockSpec(memory_space=pltpu.VMEM)] * 3,
        out_specs=pl.BlockSpec(memory_space=pltpu.VMEM),
        scratch_shapes=[
            pltpu.VMEM((2, 3, NY, 16, 256), BF),
            pltpu.VMEM((2, 256, F), BF),
            pltpu.VMEM((2, 2, 3, NY, 16, F), F32),
            *pair, *twice, *twice,
            *[pltpu.VMEM((2, 2, 48, F), F32)] * 2,
            *[pltpu.VMEM((3, 2, 48, F), BF)] * 2,
            pltpu.VMEM((3, 16, F), BF),
            *[dma((4,))] * 2, *[dma((2,))] * 2, *[dma((2, 2))] * 2,
            *[dma((2, 2, 2))] * 2, *[dma((2, 2))] * 2, *[dma((3,))] * 2,
            dma((3, 2)), dma, *[dma((NY,))] * 4,
        ],
        compiler_params=pltpu.CompilerParams(
            collective_id=0, has_side_effects=True, vmem_limit_bytes=40 << 20
        ),
        cost_estimate=pl.CostEstimate(
            flops=80_000_000_000, bytes_accessed=8_000_000, transcendentals=30720
        ),
    )(tokens.reshape(NZ, NY, 16, 256), gate_weight, up_weight)


def out_kernel(h, w, out, acc, got, ss, rs):
    xh = lax.axis_index("xh")
    barrier = pltpu.get_barrier_semaphore()
    pl.semaphore_signal(barrier, inc=1, device_id={"xh": 1 - xh}, device_id_type=MESH)
    acc[...] = dot(h[...], w[...]).reshape(2, 64, 256)
    pl.semaphore_wait(barrier, 1)
    cp = pltpu.make_async_remote_copy(
        src_ref=acc.at[1 - xh], dst_ref=got, send_sem=ss, recv_sem=rs,
        device_id={"xh": 1 - xh}, device_id_type=MESH,
    )
    cp.start()
    cp.wait()
    out[...] = (acc[xh] + got[...]).astype(BF)


def summed_out(h, w):
    dma = pltpu.SemaphoreType.DMA
    return pl.pallas_call(
        out_kernel,
        out_shape=jax.ShapeDtypeStruct((64, 256), BF),
        in_specs=[pl.BlockSpec(memory_space=pltpu.VMEM)] * 2,
        out_specs=pl.BlockSpec(memory_space=pltpu.VMEM),
        scratch_shapes=[
            pltpu.VMEM((2, 64, 256), F32), pltpu.VMEM((64, 256), F32), dma, dma,
        ],
        compiler_params=pltpu.CompilerParams(
            collective_id=1, has_side_effects=True, vmem_limit_bytes=24 << 20
        ),
    )(h, w)


def body(tokens, gate_weight, up_weight, down_weight):
    down = lax.all_gather(down_weight, "z", axis=0, tiled=True)
    hidden = gathered_hidden(tokens, gate_weight, up_weight)
    return summed_out(hidden, down)


def solution(mesh):
    split = Mesh(mesh.devices.reshape(NY, 2, 2, NZ, 2), AXES)
    in_specs = (P(None, DP), P(DP, MP), P(DP, MP), P(MP, DP))
    return jax.shard_map(body, mesh=split, in_specs=in_specs, out_specs=P(MP, DP), check_vma=False)
```

```python
import jax
import jax.numpy as jnp
from jax import lax
from jax.experimental import pallas as pl
from jax.experimental.pallas import tpu as pltpu
from jax.sharding import Mesh
from jax.sharding import PartitionSpec as P

AXES = ("y", "xl", "c", "z", "xh")
NY, NZ = 8, 12
DP = ("y", "xl", "c")
MP = ("z", "xh")
F = 640
MESH = pl.DeviceIdType.MESH
BF = jnp.bfloat16
F32 = jnp.float32


def dot(a, b):
    return jnp.dot(a, b, preferred_element_type=F32)


def block_kernel(
    tok_in, gw_in, uw_in, wd_in, out,
    tok, w_a, tok_b, w_b, part, s1s, s1r, s2s, s2r, s3s, s3r, s4s, s4r, xs, xr, hid,
    hall, down, acc, got,
    in_s, ex_s, ex_r, r1_s, r1_r, r2_s, r2_r, r3_s, r3_r, r4_s, r4_r, x_s, x_r,
    za_s, za_r, ya_s, ya_r, xa_s, xa_r, cf_s, cf_r, zr_s, zr_r, xh_s, xh_r,
):
    y, xl, c, z, xh = (lax.axis_index(a) for a in AXES)
    other_x, other_c = 1 - xl, 1 - c

    def at_y(d):
        return lax.rem(y + (d + NY), NY)

    def at_z(d):
        return lax.rem(z + (d + NZ), NZ)

    def put(src, dst, ss, rs, **where):
        return pltpu.make_async_remote_copy(
            src_ref=src, dst_ref=dst, send_sem=ss, recv_sem=rs,
            device_id=where, device_id_type=MESH,
        )

    barrier = pltpu.get_barrier_semaphore()

    def greet(**where):
        pl.semaphore_signal(barrier, inc=1, device_id=where, device_id_type=MESH)

    greet(c=other_c)
    greet(xl=other_x)
    greet(xh=1 - xh)
    for d in range(1, NY):
        greet(y=at_y(d))
    for d in (1, -1):
        greet(y=at_y(d), xl=other_x)
        greet(z=at_z(d))
    group = z // 3
    active = c == lax.rem(group, 2)
    for k in range(6):

        @pl.when(active & (z != 6 * xl + k))
        def _():
            greet(xl=group // 2, z=6 * xl + k)

    loads = [
        pltpu.make_async_copy(src, dst, in_s.at[k])
        for k, (src, dst) in enumerate(
            ((gw_in, w_a.at[0]), (uw_in, w_a.at[1]), (tok_in, tok), (wd_in, down.at[z]))
        )
    ]
    for cp in loads:
        cp.start()
    for cp in loads:
        cp.wait()
    my_first = 6 * xl + 3 * c
    mine = (z >= my_first) & (z < my_first + 3)
    pl.semaphore_wait(barrier, 3 + (NY - 1) + 4 + 3 - mine.astype(jnp.int32))

    def ring(i, h, k):
        sign = (1, -1)[i]
        block = down.at[at_z(-sign * (k - 1)), pl.ds(320 * h, 320)]
        return put(block, block, zr_s.at[i, h, k], zr_r.at[i, h, k], z=at_z(sign))

    def last(i, h):
        return 6 if i == h else 5

    def advance(k, chunks=(0, 1)):
        for h in chunks:
            for i in range(2):
                if k <= last(i, h):
                    sign = (1, -1)[i]
                    block = down.at[at_z(-sign * k), pl.ds(320 * h, 320)]
                    put(block, block, zr_s.at[i, h, k], zr_r.at[i, h, k], z=at_z(sign)).wait_recv()
                if k < last(i, h):
                    ring(i, h, k + 1).start()

    exchange = [
        put(tok.at[pl.ds(6 * h + 3 * other_c, 3)], tok_b.at[h], ex_s.at[h], ex_r.at[h], c=other_c)
        for h in range(2)
    ] + [
        put(w_a.at[k], w_b.at[k], ex_s.at[2 + k], ex_r.at[2 + k], c=other_c)
        for k in range(2)
    ]
    for cp in exchange:
        cp.start()
    for h in range(2):
        for i in range(2):
            ring(i, h, 1).start()
    for k in range(2):
        for h in range(2):
            a = tok[pl.ds(6 * h + 3 * c, 3)].reshape(384, 256)
            part[k, h] = dot(a, w_a[k]).reshape(3, NY, 16, F)
    for cp in exchange:
        cp.wait_recv()

    sent = list(exchange)

    def go(cp):
        cp.start()
        sent.append(cp)
        return cp

    def own(k, h, o):
        return part[k, h, :, o].reshape(48, F)

    far = at_y(4)
    for k in range(2):
        for h in range(2):
            a = tok_b[h, :, far].reshape(48, 256)
            s1s[k, h] = (own(k, h, far) + dot(a, w_b[k])).astype(BF)
    step1 = [
        go(put(s1s.at[k], s1r.at[k], r1_s.at[k], r1_r.at[k], y=at_y((-1, 1)[k]))) for k in range(2)
    ]
    for k in range(2):
        for h in range(2):
            a = tok_b[h].reshape(384, 256)
            part[k, h] = part[k, h] + dot(a, w_b[k]).reshape(3, NY, 16, F)

    step2 = [[None, None], [None, None]]

    def second(i, k):
        sign = (-1, 1)[i]
        for h in range(2):
            v = own(k, h, at_y(3 * sign))
            if i == k:
                v = v + s1r[k, h].astype(F32)
            s2s[i, k, h] = v.astype(BF)
        step2[i][k] = go(
            put(s2s.at[i, k], s2r.at[i, k], r2_s.at[i, k], r2_r.at[i, k], y=at_y(sign))
        )

    second(0, 1)
    second(1, 0)
    crossing = []
    for j in range(3):
        for k in range(2):
            xs[j, k] = own(k, other_x, at_y(j - 1)).astype(BF)
        crossing.append(go(put(xs.at[j], xr.at[j], x_s.at[j], x_r.at[j], xl=other_x)))
    for k in range(2):
        step1[k].wait_recv()
        second(k, k)

    advance(1)

    step3 = {}
    for i, k in ((0, 1), (1, 0), (0, 0), (1, 1)):
        sign = (-1, 1)[i]
        step2[i][k].wait_recv()
        for h in range(2):
            s3s[i, k, h] = (own(k, h, at_y(2 * sign)) + s2r[i, k, h].astype(F32)).astype(BF)
        for t, where in ((0, xl), (1, other_x)):
            step3[i, k, t] = go(
                put(
                    s3s.at[i, k, where], s3r.at[i, k, t], r3_s.at[i, k, t], r3_r.at[i, k, t],
                    y=at_y(sign), xl=where,
                )
            )

    advance(2)

    step4 = {}
    crossing[0].wait_recv()
    crossing[2].wait_recv()
    for i, k in ((0, 1), (1, 0), (0, 0), (1, 1)):
        sign = (-1, 1)[i]
        for t in range(2):
            step3[i, k, t].wait_recv()
        s4s[i, k] = (
            own(k, xl, at_y(sign))
            + s3r[i, k, 0].astype(F32)
            + s3r[i, k, 1].astype(F32)
            + xr[1 + sign, k].astype(F32)
        )
        step4[i, k] = go(
            put(s4s.at[i, k], s4r.at[i, k], r4_s.at[i, k], r4_r.at[i, k], y=at_y(sign))
        )
    advance(3)
    crossing[1].wait_recv()
    total = []
    for k in range(2):
        for i in range(2):
            step4[i, k].wait_recv()
        total.append(own(k, xl, y) + s4r[0, k] + s4r[1, k] + xr[1, k].astype(F32))
    hid[...] = (jax.nn.silu(total[0]) * total[1]).astype(BF).reshape(3, 16, F)

    def piece(d, x):
        row = pl.multiple_of(16 * at_y(-d), 16)
        return hall.at[pl.ds(row, 16), pl.ds(pl.multiple_of(6 * F * x, 128), 6 * F)]

    to_x = z // 6
    row = pl.multiple_of(16 * y, 16)
    slot = hall.at[pl.ds(row, 16), pl.ds(pl.multiple_of(z * F, 128), F)]

    def along_z(j):
        return put(hid.at[j], slot, za_s.at[j], za_r, z=my_first + j, xl=to_x)

    for j in range(3):

        @pl.when(my_first + j != z)
        def _():
            along_z(j).start()

        @pl.when(my_first + j == z)
        def _():
            pltpu.make_async_copy(hid.at[j], slot, za_r).start()

    advance(4)

    order = (1, 7, 2, 6, 3, 5, 4)

    def along_y(d):
        own_piece = piece(0, xl)
        return put(own_piece, own_piece, ya_s.at[d], ya_r.at[d], y=at_y(d))

    def across(d):
        return put(piece(d, xl), piece(d, xl), xa_s.at[d], xa_r.at[d], xl=other_x)

    def to_core(d, t):
        p = piece(d, xl if t == 0 else other_x)
        return put(p, p, cf_s.at[t, d], cf_r.at[t, d], c=other_c)

    @pl.when(active)
    def _():
        pltpu.make_async_copy(piece(0, xl), piece(0, xl), za_r).wait()
        for d in order:
            along_y(d).start()
        across(0).start()
        to_core(0, 0).start()

    advance(5)

    def came_across(d):
        p = piece(d, other_x)
        put(p, p, xa_s.at[d], xa_r.at[d], xl=other_x).wait_recv()
        to_core(d, 1).start()

    @pl.when(active)
    def _():
        late = (0, *order)
        for n, d in enumerate(order):
            p = piece(d, xl)
            put(p, p, ya_s.at[d], ya_r.at[d], y=at_y(d)).wait_recv()
            across(d).start()
            to_core(d, 0).start()
            if n >= 2:
                came_across(late[n - 2])
        for d in late[5:]:
            came_across(d)

    @pl.when(jnp.logical_not(active))
    def _():
        for d in (0, *order):
            for t in range(2):
                to_core(d, t).wait_recv()

    advance(6)

    def rows_of(t):
        lhs = hall[pl.ds(pl.multiple_of(64 * t, 64), 64), :]
        return dot(lhs, down[...].reshape(NZ * F, 256))

    acc[...] = rows_of(1 - xh)
    final = put(acc, got, xh_s, xh_r, xh=1 - xh)
    final.start()
    result = rows_of(xh)
    final.wait_recv()
    out[...] = (result + got[...]).astype(BF)

    final.wait_send()
    for j in range(3):

        @pl.when(my_first + j != z)
        def _():
            along_z(j).wait_send()

    @pl.when(active)
    def _():
        for d in order:
            along_y(d).wait_send()
        for d in (0, *order):
            across(d).wait_send()
            for t in range(2):
                to_core(d, t).wait_send()

    for h in range(2):
        for i in range(2):
            for k in range(1, last(i, h) + 1):
                ring(i, h, k).wait_send()
    for cp in sent:
        cp.wait_send()


def body(tokens, gate_weight, up_weight, down_weight):
    dma = pltpu.SemaphoreType.DMA
    twice = [pltpu.VMEM((2, 2, 2, 48, F), BF)] * 2
    return pl.pallas_call(
        block_kernel,
        out_shape=jax.ShapeDtypeStruct((64, 256), BF),
        in_specs=[pl.BlockSpec(memory_space=pl.ANY)] * 4,
        out_specs=pl.BlockSpec(memory_space=pltpu.VMEM),
        scratch_shapes=[
            pltpu.VMEM((NZ, NY, 16, 256), BF),
            pltpu.VMEM((2, 256, F), BF),
            pltpu.VMEM((2, 3, NY, 16, 256), BF),
            pltpu.VMEM((2, 256, F), BF),
            pltpu.VMEM((2, 2, 3, NY, 16, F), F32),
            *[pltpu.VMEM((2, 2, 48, F), BF)] * 2, *twice, *twice,
            *[pltpu.VMEM((2, 2, 48, F), F32)] * 2,
            *[pltpu.VMEM((3, 2, 48, F), BF)] * 2,
            pltpu.VMEM((3, 16, F), BF),
            pltpu.VMEM((16 * NY, NZ * F), BF),
            pltpu.VMEM((NZ, F, 256), BF),
            *[pltpu.VMEM((64, 256), F32)] * 2,
            dma((4,)),
            *[dma((4,))] * 2, *[dma((2,))] * 2, *[dma((2, 2))] * 2,
            *[dma((2, 2, 2))] * 2, *[dma((2, 2))] * 2, *[dma((3,))] * 2,
            dma((3,)), dma, *[dma((NY,))] * 4, *[dma((2, NY))] * 2,
            *[dma((2, 2, 7))] * 2, dma, dma,
        ],
        compiler_params=pltpu.CompilerParams(
            collective_id=0, has_side_effects=True, vmem_limit_bytes=60 << 20
        ),
    )(tokens.reshape(NZ, NY, 16, 256), gate_weight, up_weight, down_weight)


def solution(mesh):
    split = Mesh(mesh.devices.reshape(NY, 2, 2, NZ, 2), AXES)
    in_specs = (P(None, DP), P(DP, MP), P(DP, MP), P(MP, DP))
    return jax.shard_map(body, mesh=split, in_specs=in_specs, out_specs=P(MP, DP), check_vma=False)
```

```python
import jax
import jax.numpy as jnp
from jax import lax
from jax.experimental import pallas as pl
from jax.experimental.pallas import tpu as pltpu
from jax.sharding import Mesh
from jax.sharding import PartitionSpec as P

AXES = ("y", "xl", "c", "z", "xh")
NY, NZ = 8, 12
WHEN = {
    ('third', 0): ((1, 0),),
    ('third', 1): ((1, 1),),
    ('fourth', 0): ((2, 0),),
    ('fourth', 1): ((2, 1),),
    ('hidden', 0): ((3, 0),),
    ('hidden', 1): ((3, 1),),
    ('gather', 0): ((4, 0),),
    ('gather', 1): ((4, 1),),
    ('pass', 4): ((5, 0),),
    ('pass', 7): ((5, 1),),
    ('last', 0): ((6, 0), (6, 1)),
}
DP = ("y", "xl", "c")
MP = ("z", "xh")
F = 640
CHUNKS = ((0, 256), (256, 384))
MESH = pl.DeviceIdType.MESH
BF = jnp.bfloat16
F32 = jnp.float32


def dot(a, b):
    return jnp.dot(a, b, preferred_element_type=F32)


def block_kernel(
    tok_in, gw_in, uw_in, wd_in, out,
    tok, w_a, tok_b, w_b, part, xs, xr, down, acc, got, ring_bufs,
    in_s, ex_s, ex_r, r1_s, r1_r, r2_s, r2_r, r3_s, r3_r, r4_s, r4_r, x_s, x_r,
    za_s, za_r, ya_s, ya_r, xa_s, xa_r, cf_s, cf_r, zr_s, zr_r, xh_s, xh_r,
):
    y, xl, c, z, xh = (lax.axis_index(a) for a in AXES)
    other_x, other_c = 1 - xl, 1 - c

    def at_y(d):
        return lax.rem(y + (d + NY), NY)

    def at_z(d):
        return lax.rem(z + (d + NZ), NZ)

    def put(src, dst, ss, rs, **where):
        return pltpu.make_async_remote_copy(
            src_ref=src, dst_ref=dst, send_sem=ss, recv_sem=rs,
            device_id=where, device_id_type=MESH,
        )

    barrier = pltpu.get_barrier_semaphore()

    def greet(**where):
        pl.semaphore_signal(barrier, inc=1, device_id=where, device_id_type=MESH)

    greet(c=other_c)
    greet(xl=other_x)
    greet(xh=1 - xh)
    for d in range(1, NY):
        greet(y=at_y(d))
    for d in (1, -1):
        greet(y=at_y(d), xl=other_x)
        greet(z=at_z(d))
    group = z // 3
    active = c == lax.rem(group, 2)
    for k in range(6):

        @pl.when(active & (z != 6 * xl + k))
        def _():
            greet(xl=group // 2, z=6 * xl + k)

    loads = [
        pltpu.make_async_copy(src, dst, in_s.at[k])
        for k, (src, dst) in enumerate(
            ((gw_in, w_a.at[0]), (uw_in, w_a.at[1]), (tok_in, tok), (wd_in, down.at[z]))
        )
    ]
    for cp in loads:
        cp.start()
    for cp in loads:
        cp.wait()
    my_first = 6 * xl + 3 * c
    mine = (z >= my_first) & (z < my_first + 3)
    pl.semaphore_wait(barrier, 3 + (NY - 1) + 4 + 3 - mine.astype(jnp.int32))

    def ring(i, h, k):
        sign = (1, -1)[i]
        block = down.at[at_z(-sign * (k - 1)), pl.ds(320 * h, 320)]
        return put(block, block, zr_s.at[i, h, k], zr_r.at[i, h, k], z=at_z(sign))

    def last(i, h):
        return 6 if i == h else 5

    def advance(k, h):
        for i in range(2):
            if k <= last(i, h):
                sign = (1, -1)[i]
                block = down.at[at_z(-sign * k), pl.ds(320 * h, 320)]
                put(block, block, zr_s.at[i, h, k], zr_r.at[i, h, k], z=at_z(sign)).wait_recv()
            if k < last(i, h):
                ring(i, h, k + 1).start()

    def onward(stage, n):
        for k, h in WHEN.get((stage, n), ()):
            advance(k, h)

    exchange = [
        put(tok.at[pl.ds(6 * h + 3 * other_c, 3)], tok_b.at[h], ex_s.at[h], ex_r.at[h], c=other_c)
        for h in range(2)
    ] + [
        put(w_a.at[k], w_b.at[k], ex_s.at[2 + k], ex_r.at[2 + k], c=other_c)
        for k in range(2)
    ]
    for cp in exchange:
        cp.start()
    for h in range(2):
        for i in range(2):
            ring(i, h, 1).start()
    for k in range(2):
        for h in range(2):
            a = tok[pl.ds(6 * h + 3 * c, 3)].reshape(384, 256)
            part[k, h] = dot(a, w_a[k]).reshape(3, NY, 16, F)
    for cp in exchange:
        cp.wait_recv()

    sent = list(exchange)

    def go(cp):
        cp.start()
        sent.append(cp)
        return cp

    def own(k, h, o):
        return part[k, h, :, o].reshape(48, F)

    def cols(n):
        return pl.ds(CHUNKS[n][0], CHUNKS[n][1])

    def own_cols(k, h, o, n):
        return part[k, h, :, o, :, cols(n)].reshape(48, CHUNKS[n][1])

    def bufs(n):
        return ring_bufs[n]

    def long_way(n):
        return n % 2

    step1, step2, step3, step4 = {}, {}, {}, {}
    many = range(len(CHUNKS))
    far = at_y(4)
    for n in many:
        s1s, s1r = bufs(n)[0:2]
        for k in range(2):
            for h in range(2):
                a = tok_b[h, :, far].reshape(48, 256)
                s1s[h, k] = (own_cols(k, h, far, n) + dot(a, w_b[k, :, cols(n)])).astype(BF)
        step1[n] = go(
            put(s1s, s1r, r1_s.at[n], r1_r.at[n], y=at_y((-1, 1)[long_way(n)]))
        )
    for k in range(2):
        for h in range(2):
            a = tok_b[h].reshape(384, 256)
            part[k, h] = part[k, h] + dot(a, w_b[k]).reshape(3, NY, 16, F)

    def second(n, i):
        s1r, s2s, s2r = bufs(n)[1:4]
        sign = (-1, 1)[i]
        for k in range(2):
            for h in range(2):
                v = own_cols(k, h, at_y(3 * sign), n)
                if i == long_way(n):
                    v = v + s1r[h, k].astype(F32)
                s2s[i, h, k] = v.astype(BF)
        step2[n, i] = go(
            put(s2s.at[i], s2r.at[i], r2_s.at[n, i], r2_r.at[n, i], y=at_y(sign))
        )

    for n in many:
        second(n, 1 - long_way(n))
    crossing = []
    for j in range(3):
        for k in range(2):
            xs[j, k] = own(k, other_x, at_y(j - 1)).astype(BF)
        crossing.append(go(put(xs.at[j], xr.at[j], x_s.at[j], x_r.at[j], xl=other_x)))
    for n in many:
        step1[n].wait_recv()
        second(n, long_way(n))
        onward('second', n)

    def third(n, i):
        s2r, s3s, s3r = bufs(n)[3:6]
        sign = (-1, 1)[i]
        step2[n, i].wait_recv()
        for k in range(2):
            for h in range(2):
                s3s[i, h, k] = (
                    own_cols(k, h, at_y(2 * sign), n) + s2r[i, h, k].astype(F32)
                ).astype(BF)
        for t, where in ((0, xl), (1, other_x)):
            step3[n, i, t] = go(
                put(
                    s3s.at[i, where], s3r.at[i, t], r3_s.at[n, i, t], r3_r.at[n, i, t],
                    y=at_y(sign), xl=where,
                )
            )

    for n in many:
        third(n, 1 - long_way(n))
        third(n, long_way(n))
        onward('third', n)

    crossing[0].wait_recv()
    crossing[2].wait_recv()

    def fourth(n, i):
        s3r, s4s, s4r = bufs(n)[5:8]
        sign = (-1, 1)[i]
        for t in range(2):
            step3[n, i, t].wait_recv()
        for k in range(2):
            s4s[i, k] = (
                own_cols(k, xl, at_y(sign), n)
                + s3r[i, 0, k].astype(F32)
                + s3r[i, 1, k].astype(F32)
                + xr[1 + sign, k, :, cols(n)].astype(F32)
            )
        step4[n, i] = go(
            put(s4s.at[i], s4r.at[i], r4_s.at[n, i], r4_r.at[n, i], y=at_y(sign))
        )

    for n in many:
        fourth(n, 1 - long_way(n))
        fourth(n, long_way(n))
        onward('fourth', n)
    crossing[1].wait_recv()

    to_x = z // 6
    row = pl.multiple_of(16 * y, 16)

    def slot(n):
        w = CHUNKS[n][1]
        return bufs(n)[9].at[pl.ds(row, 16), pl.ds(pl.multiple_of(z * w, 128), w)]

    def along_z(n, j):
        return put(
            bufs(n)[8].at[j], slot(n), za_s.at[n, j], za_r.at[n], z=my_first + j, xl=to_x
        )

    for n in many:
        s4r, hid = bufs(n)[7:9]
        for i in range(2):
            step4[n, i].wait_recv()
        gate, up = (
            own_cols(k, xl, y, n) + s4r[0, k] + s4r[1, k] + xr[1, k, :, cols(n)].astype(F32)
            for k in range(2)
        )
        hid[...] = (jax.nn.silu(gate) * up).astype(BF).reshape(hid.shape)
        for j in range(3):

            @pl.when(my_first + j != z)
            def _():
                along_z(n, j).start()

            @pl.when(my_first + j == z)
            def _():
                pltpu.make_async_copy(hid.at[j], slot(n), za_r.at[n]).start()

        onward('hidden', n)


    order = (1, 7, 2, 6, 3, 5, 4)

    def piece(n, d, x):
        start = pl.multiple_of(16 * at_y(-d), 16)
        w = 6 * CHUNKS[n][1]
        return bufs(n)[9].at[pl.ds(start, 16), pl.ds(pl.multiple_of(w * x, 128), w)]

    def along_y(n, d):
        p = piece(n, 0, xl)
        return put(p, p, ya_s.at[n, d], ya_r.at[n, d], y=at_y(d))

    def across(n, d):
        p = piece(n, d, xl)
        return put(p, p, xa_s.at[n, d], xa_r.at[n, d], xl=other_x)

    def to_core(n, d, t):
        p = piece(n, d, xl if t == 0 else other_x)
        return put(p, p, cf_s.at[n, t, d], cf_r.at[n, t, d], c=other_c)

    for n in many:

        @pl.when(active)
        def _():
            p = piece(n, 0, xl)
            pltpu.make_async_copy(p, p, za_r.at[n]).wait()
            for d in order:
                along_y(n, d).start()
            across(n, 0).start()
            to_core(n, 0, 0).start()

        onward('gather', n)

    def came_along(n, d):
        p = piece(n, d, xl)
        put(p, p, ya_s.at[n, d], ya_r.at[n, d], y=at_y(d)).wait_recv()
        across(n, d).start()
        to_core(n, d, 0).start()

    def came_across(n, d):
        p = piece(n, d, other_x)
        put(p, p, xa_s.at[n, d], xa_r.at[n, d], xl=other_x).wait_recv()
        to_core(n, d, 1).start()

    events = [(n, d) for n in many for d in order]
    crossed = [(n, d) for n in many for d in (0, *order)]

    def order_of(d):
        return (0, *order).index(d) - 1

    @pl.when(active)
    def _():
        done = 0
        for count, (n, d) in enumerate(events):
            came_along(n, d)
            while done < len(crossed) and crossed[done][0] * 7 + order_of(crossed[done][1]) + 4 < count:
                came_across(*crossed[done])
                done += 1
            onward('pass', count)
        for at in crossed[done:]:
            came_across(*at)

    @pl.when(jnp.logical_not(active))
    def _():
        for count, (n, d) in enumerate(crossed):
            for t in range(2):
                to_core(n, d, t).wait_recv()
            onward('pass', count)

    onward('last', 0)

    def rows_of(t):
        r = pl.ds(pl.multiple_of(64 * t, 64), 64)
        return sum(
            dot(bufs(n)[9][r, :], down[:, cols(n), :].reshape(NZ * CHUNKS[n][1], 256))
            for n in many
        )

    acc[...] = rows_of(1 - xh)
    final = put(acc, got, xh_s, xh_r, xh=1 - xh)
    final.start()
    result = rows_of(xh)
    final.wait_recv()
    out[...] = (result + got[...]).astype(BF)

    final.wait_send()
    for n in many:
        for j in range(3):

            @pl.when(my_first + j != z)
            def _():
                along_z(n, j).wait_send()

    @pl.when(active)
    def _():
        for n in many:
            for d in order:
                along_y(n, d).wait_send()
            for d in (0, *order):
                across(n, d).wait_send()
                for t in range(2):
                    to_core(n, d, t).wait_send()

    for h in range(2):
        for i in range(2):
            for k in range(1, last(i, h) + 1):
                ring(i, h, k).wait_send()
    for cp in sent:
        cp.wait_send()


def body(tokens, gate_weight, up_weight, down_weight):
    dma = pltpu.SemaphoreType.DMA
    m = len(CHUNKS)

    def chunk_bufs(w):
        return [
            *[pltpu.VMEM((2, 2, 48, w), BF)] * 2,
            *[pltpu.VMEM((2, 2, 2, 48, w), BF)] * 4,
            *[pltpu.VMEM((2, 2, 48, w), F32)] * 2,
            pltpu.VMEM((3, 16, w), BF),
            pltpu.VMEM((16 * NY, NZ * w), BF),
        ]

    return pl.pallas_call(
        block_kernel,
        out_shape=jax.ShapeDtypeStruct((64, 256), BF),
        in_specs=[pl.BlockSpec(memory_space=pltpu.HBM)] * 4,
        out_specs=pl.BlockSpec(memory_space=pltpu.VMEM),
        scratch_shapes=[
            pltpu.VMEM((NZ, NY, 16, 256), BF),
            pltpu.VMEM((2, 256, F), BF),
            pltpu.VMEM((2, 3, NY, 16, 256), BF),
            pltpu.VMEM((2, 256, F), BF),
            pltpu.VMEM((2, 2, 3, NY, 16, F), F32),
            *[pltpu.VMEM((3, 2, 48, F), BF)] * 2,
            pltpu.VMEM((NZ, F, 256), BF),
            *[pltpu.VMEM((64, 256), F32)] * 2,
            [chunk_bufs(w) for _, w in CHUNKS],
            dma((4,)),
            *[dma((4,))] * 2, *[dma((m,))] * 2, *[dma((m, 2))] * 2,
            *[dma((m, 2, 2))] * 2, *[dma((m, 2))] * 2, *[dma((3,))] * 2,
            dma((m, 3)), dma((m,)), *[dma((m, NY))] * 4, *[dma((m, 2, NY))] * 2,
            *[dma((2, 2, 7))] * 2, dma, dma,
        ],
        compiler_params=pltpu.CompilerParams(
            collective_id=0, has_side_effects=True, vmem_limit_bytes=55040 << 10
        ),
    )(tokens.reshape(NZ, NY, 16, 256), gate_weight, up_weight, down_weight)


def solution(mesh):
    split = Mesh(mesh.devices.reshape(NY, 2, 2, NZ, 2), AXES)
    in_specs = (P(None, DP), P(DP, MP), P(DP, MP), P(MP, DP))
    return jax.shard_map(body, mesh=split, in_specs=in_specs, out_specs=P(MP, DP), check_vma=False)
```

```python
import jax
import jax.numpy as jnp
from jax import lax
from jax.experimental import pallas as pl
from jax.experimental.pallas import tpu as pltpu
from jax.sharding import Mesh
from jax.sharding import PartitionSpec as P

AXES = ("y", "xl", "c", "z", "xh")
NY, NZ = 8, 12
WHEN = {
    ('second', 1): ((1, 0),),
    ('third', 0): ((1, 1),),
    ('third', 1): ((2, 0),),
    ('fourth', 0): ((2, 1),),
    ('fourth', 1): ((3, 0),),
    ('hidden', 0): ((3, 1),),
    ('hidden', 1): ((4, 0),),
    ('gather', 0): ((4, 1),),
    ('pass', 1): ((5, 0),),
    ('pass', 5): ((5, 1),),
    ('pass', 9): ((6, 0),),
    ('last', 0): ((6, 1),),
}
DP = ("y", "xl", "c")
MP = ("z", "xh")
F = 640
CHUNKS = ((0, 256), (256, 384))
MESH = pl.DeviceIdType.MESH
BF = jnp.bfloat16
F32 = jnp.float32


def dot(a, b):
    return jnp.dot(a, b, preferred_element_type=F32)


def block_kernel(
    tok_in, gw_in, uw_in, wd_in, out,
    tok, w_a, tok_b, w_b, part, xs, xr, down, acc, got, ring_bufs,
    in_s, ex_s, ex_r, r1_s, r1_r, r2_s, r2_r, r3_s, r3_r, r4_s, r4_r, x_s, x_r,
    za_s, za_r, ya_s, ya_r, xa_s, xa_r, cf_s, cf_r, zr_s, zr_r, xh_s, xh_r,
):
    y, xl, c, z, xh = (lax.axis_index(a) for a in AXES)
    other_x, other_c = 1 - xl, 1 - c

    def at_y(d):
        return lax.rem(y + (d + NY), NY)

    def at_z(d):
        return lax.rem(z + (d + NZ), NZ)

    def put(src, dst, ss, rs, **where):
        return pltpu.make_async_remote_copy(
            src_ref=src, dst_ref=dst, send_sem=ss, recv_sem=rs,
            device_id=where, device_id_type=MESH,
        )

    barrier = pltpu.get_barrier_semaphore()

    def greet(**where):
        pl.semaphore_signal(barrier, inc=1, device_id=where, device_id_type=MESH)

    greet(c=other_c)
    greet(xl=other_x)
    greet(xh=1 - xh)
    for d in range(1, NY):
        greet(y=at_y(d))
    for d in (1, -1):
        greet(y=at_y(d), xl=other_x)
        greet(z=at_z(d))
    group = z // 3
    active = c == lax.rem(group, 2)
    for k in range(6):

        @pl.when(active & (z != 6 * xl + k))
        def _():
            greet(xl=group // 2, z=6 * xl + k)

    loads = [
        pltpu.make_async_copy(src, dst, in_s.at[k])
        for k, (src, dst) in enumerate(
            ((gw_in, w_a.at[0]), (uw_in, w_a.at[1]), (tok_in, tok), (wd_in, down.at[z]))
        )
    ]
    for cp in loads:
        cp.start()
    for cp in loads:
        cp.wait()
    my_first = 6 * xl + 3 * c
    mine = (z >= my_first) & (z < my_first + 3)
    pl.semaphore_wait(barrier, 3 + (NY - 1) + 4 + 3 - mine.astype(jnp.int32))

    def ring(i, h, k):
        sign = (1, -1)[i]
        block = down.at[at_z(-sign * (k - 1)), pl.ds(320 * h, 320)]
        return put(block, block, zr_s.at[i, h, k], zr_r.at[i, h, k], z=at_z(sign))

    def last(i, h):
        return 6 if i == h else 5

    def advance(k, h):
        for i in range(2):
            if k <= last(i, h):
                sign = (1, -1)[i]
                block = down.at[at_z(-sign * k), pl.ds(320 * h, 320)]
                put(block, block, zr_s.at[i, h, k], zr_r.at[i, h, k], z=at_z(sign)).wait_recv()
            if k < last(i, h):
                ring(i, h, k + 1).start()

    def onward(stage, n):
        for k, h in WHEN.get((stage, n), ()):
            advance(k, h)

    exchange = [
        put(tok.at[pl.ds(6 * h + 3 * other_c, 3)], tok_b.at[h], ex_s.at[h], ex_r.at[h], c=other_c)
        for h in range(2)
    ] + [
        put(w_a.at[k], w_b.at[k], ex_s.at[2 + k], ex_r.at[2 + k], c=other_c)
        for k in range(2)
    ]
    for cp in exchange:
        cp.start()
    for h in range(2):
        for i in range(2):
            ring(i, h, 1).start()
    for k in range(2):
        for h in range(2):
            a = tok[pl.ds(6 * h + 3 * c, 3)].reshape(384, 256)
            part[k, h] = dot(a, w_a[k]).reshape(3, NY, 16, F)
    for cp in exchange:
        cp.wait_recv()

    sent = list(exchange)

    def go(cp):
        cp.start()
        sent.append(cp)
        return cp

    def own(k, h, o):
        return part[k, h, :, o].reshape(48, F)

    def cols(n):
        return pl.ds(CHUNKS[n][0], CHUNKS[n][1])

    def own_cols(k, h, o, n):
        return part[k, h, :, o, :, cols(n)].reshape(48, CHUNKS[n][1])

    def bufs(n):
        return ring_bufs[n]

    def long_way(n):
        return n % 2

    step1, step2, step3, step4 = {}, {}, {}, {}
    many = range(len(CHUNKS))
    far = at_y(4)
    for n in many:
        s1s, s1r = bufs(n)[0:2]
        for k in range(2):
            for h in range(2):
                a = tok_b[h, :, far].reshape(48, 256)
                s1s[h, k] = (own_cols(k, h, far, n) + dot(a, w_b[k, :, cols(n)])).astype(BF)
        step1[n] = go(
            put(s1s, s1r, r1_s.at[n], r1_r.at[n], y=at_y((-1, 1)[long_way(n)]))
        )
    for k in range(2):
        for h in range(2):
            a = tok_b[h].reshape(384, 256)
            part[k, h] = part[k, h] + dot(a, w_b[k]).reshape(3, NY, 16, F)

    def second(n, i):
        s1r, s2s, s2r = bufs(n)[1:4]
        sign = (-1, 1)[i]
        for k in range(2):
            for h in range(2):
                v = own_cols(k, h, at_y(3 * sign), n)
                if i == long_way(n):
                    v = v + s1r[h, k].astype(F32)
                s2s[i, h, k] = v.astype(BF)
        step2[n, i] = go(
            put(s2s.at[i], s2r.at[i], r2_s.at[n, i], r2_r.at[n, i], y=at_y(sign))
        )

    for n in many:
        second(n, 1 - long_way(n))
    crossing = []
    for j in range(3):
        for k in range(2):
            xs[j, k] = own(k, other_x, at_y(j - 1)).astype(BF)
        crossing.append(go(put(xs.at[j], xr.at[j], x_s.at[j], x_r.at[j], xl=other_x)))
    for n in many:
        step1[n].wait_recv()
        second(n, long_way(n))
        onward('second', n)

    def third(n, i):
        s2r, s3s, s3r = bufs(n)[3:6]
        sign = (-1, 1)[i]
        step2[n, i].wait_recv()
        for k in range(2):
            for h in range(2):
                s3s[i, h, k] = (
                    own_cols(k, h, at_y(2 * sign), n) + s2r[i, h, k].astype(F32)
                ).astype(BF)
        for t, where in ((0, xl), (1, other_x)):
            step3[n, i, t] = go(
                put(
                    s3s.at[i, where], s3r.at[i, t], r3_s.at[n, i, t], r3_r.at[n, i, t],
                    y=at_y(sign), xl=where,
                )
            )

    for n in many:
        third(n, 1 - long_way(n))
        third(n, long_way(n))
        onward('third', n)

    crossing[0].wait_recv()
    crossing[2].wait_recv()

    def fourth(n, i):
        s3r, s4s, s4r = bufs(n)[5:8]
        sign = (-1, 1)[i]
        for t in range(2):
            step3[n, i, t].wait_recv()
        for k in range(2):
            s4s[i, k] = (
                own_cols(k, xl, at_y(sign), n)
                + s3r[i, 0, k].astype(F32)
                + s3r[i, 1, k].astype(F32)
                + xr[1 + sign, k, :, cols(n)].astype(F32)
            )
        step4[n, i] = go(
            put(s4s.at[i], s4r.at[i], r4_s.at[n, i], r4_r.at[n, i], y=at_y(sign))
        )

    for n in many:
        fourth(n, 1 - long_way(n))
        fourth(n, long_way(n))
        onward('fourth', n)
    crossing[1].wait_recv()

    to_x = z // 6
    row = pl.multiple_of(16 * y, 16)

    def slot(n):
        w = CHUNKS[n][1]
        return bufs(n)[9].at[pl.ds(row, 16), pl.ds(pl.multiple_of(z * w, 128), w)]

    def along_z(n, j):
        return put(
            bufs(n)[8].at[j], slot(n), za_s.at[n, j], za_r.at[n], z=my_first + j, xl=to_x
        )

    for n in many:
        s4r, hid = bufs(n)[7:9]
        for i in range(2):
            step4[n, i].wait_recv()
        gate, up = (
            own_cols(k, xl, y, n) + s4r[0, k] + s4r[1, k] + xr[1, k, :, cols(n)].astype(F32)
            for k in range(2)
        )
        hid[...] = (jax.nn.silu(gate) * up).astype(BF).reshape(hid.shape)
        for j in range(3):

            @pl.when(my_first + j != z)
            def _():
                along_z(n, j).start()

            @pl.when(my_first + j == z)
            def _():
                pltpu.make_async_copy(hid.at[j], slot(n), za_r.at[n]).start()

        onward('hidden', n)


    order = (1, 7, 2, 6, 3, 5, 4)

    def piece(n, d, x):
        start = pl.multiple_of(16 * at_y(-d), 16)
        w = 6 * CHUNKS[n][1]
        return bufs(n)[9].at[pl.ds(start, 16), pl.ds(pl.multiple_of(w * x, 128), w)]

    def along_y(n, d):
        p = piece(n, 0, xl)
        return put(p, p, ya_s.at[n, d], ya_r.at[n, d], y=at_y(d))

    def across(n, d):
        p = piece(n, d, xl)
        return put(p, p, xa_s.at[n, d], xa_r.at[n, d], xl=other_x)

    def to_core(n, d, t):
        p = piece(n, d, xl if t == 0 else other_x)
        return put(p, p, cf_s.at[n, t, d], cf_r.at[n, t, d], c=other_c)

    for n in many:

        @pl.when(active)
        def _():
            p = piece(n, 0, xl)
            pltpu.make_async_copy(p, p, za_r.at[n]).wait()
            for d in order:
                along_y(n, d).start()
            across(n, 0).start()
            to_core(n, 0, 0).start()

        onward('gather', n)

    def came_along(n, d):
        p = piece(n, d, xl)
        put(p, p, ya_s.at[n, d], ya_r.at[n, d], y=at_y(d)).wait_recv()
        across(n, d).start()
        to_core(n, d, 0).start()

    def came_across(n, d):
        p = piece(n, d, other_x)
        put(p, p, xa_s.at[n, d], xa_r.at[n, d], xl=other_x).wait_recv()
        to_core(n, d, 1).start()

    events = [(n, d) for n in many for d in order]
    crossed = [(n, d) for n in many for d in (0, *order)]

    def order_of(d):
        return (0, *order).index(d) - 1

    @pl.when(active)
    def _():
        done = 0
        for count, (n, d) in enumerate(events):
            came_along(n, d)
            while done < len(crossed) and crossed[done][0] * 7 + order_of(crossed[done][1]) + 4 < count:
                came_across(*crossed[done])
                done += 1
            onward('pass', count)
        for at in crossed[done:]:
            came_across(*at)

    @pl.when(jnp.logical_not(active))
    def _():
        for count, (n, d) in enumerate(crossed):
            for t in range(2):
                to_core(n, d, t).wait_recv()
            onward('pass', count)

    onward('last', 0)

    def rows_of(t):
        r = pl.ds(pl.multiple_of(64 * t, 64), 64)
        return sum(
            dot(bufs(n)[9][r, :], down[:, cols(n), :].reshape(NZ * CHUNKS[n][1], 256))
            for n in many
        )

    acc[...] = rows_of(1 - xh)
    final = put(acc, got, xh_s, xh_r, xh=1 - xh)
    final.start()
    result = rows_of(xh)
    final.wait_recv()
    out[...] = (result + got[...]).astype(BF)

    final.wait_send()
    for n in many:
        for j in range(3):

            @pl.when(my_first + j != z)
            def _():
                along_z(n, j).wait_send()

    @pl.when(active)
    def _():
        for n in many:
            for d in order:
                along_y(n, d).wait_send()
            for d in (0, *order):
                across(n, d).wait_send()
                for t in range(2):
                    to_core(n, d, t).wait_send()

    for h in range(2):
        for i in range(2):
            for k in range(1, last(i, h) + 1):
                ring(i, h, k).wait_send()
    for cp in sent:
        cp.wait_send()


def body(tokens, gate_weight, up_weight, down_weight):
    dma = pltpu.SemaphoreType.DMA
    m = len(CHUNKS)

    def chunk_bufs(w):
        return [
            *[pltpu.VMEM((2, 2, 48, w), BF)] * 2,
            *[pltpu.VMEM((2, 2, 2, 48, w), BF)] * 4,
            *[pltpu.VMEM((2, 2, 48, w), F32)] * 2,
            pltpu.VMEM((3, 16, w), BF),
            pltpu.VMEM((16 * NY, NZ * w), BF),
        ]

    return pl.pallas_call(
        block_kernel,
        out_shape=jax.ShapeDtypeStruct((64, 256), BF),
        in_specs=[pl.BlockSpec(memory_space=pltpu.HBM)] * 4,
        out_specs=pl.BlockSpec(memory_space=pltpu.VMEM),
        scratch_shapes=[
            pltpu.VMEM((NZ, NY, 16, 256), BF),
            pltpu.VMEM((2, 256, F), BF),
            pltpu.VMEM((2, 3, NY, 16, 256), BF),
            pltpu.VMEM((2, 256, F), BF),
            pltpu.VMEM((2, 2, 3, NY, 16, F), F32),
            *[pltpu.VMEM((3, 2, 48, F), BF)] * 2,
            pltpu.VMEM((NZ, F, 256), BF),
            *[pltpu.VMEM((64, 256), F32)] * 2,
            [chunk_bufs(w) for _, w in CHUNKS],
            dma((4,)),
            *[dma((4,))] * 2, *[dma((m,))] * 2, *[dma((m, 2))] * 2,
            *[dma((m, 2, 2))] * 2, *[dma((m, 2))] * 2, *[dma((3,))] * 2,
            dma((m, 3)), dma((m,)), *[dma((m, NY))] * 4, *[dma((m, 2, NY))] * 2,
            *[dma((2, 2, 7))] * 2, dma, dma,
        ],
        compiler_params=pltpu.CompilerParams(
            collective_id=0, has_side_effects=True, vmem_limit_bytes=55040 << 10
        ),
    )(tokens.reshape(NZ, NY, 16, 256), gate_weight, up_weight, down_weight)


def solution(mesh):
    split = Mesh(mesh.devices.reshape(NY, 2, 2, NZ, 2), AXES)
    in_specs = (P(None, DP), P(DP, MP), P(DP, MP), P(MP, DP))
    return jax.shard_map(body, mesh=split, in_specs=in_specs, out_specs=P(MP, DP), check_vma=False)
```

```python
import jax
import jax.numpy as jnp
from jax import lax
from jax.experimental import pallas as pl
from jax.experimental.pallas import tpu as pltpu
from jax.sharding import Mesh
from jax.sharding import PartitionSpec as P

AXES = ("y", "xl", "c", "z", "xh")
NY, NZ = 8, 12
WHEN = {
    ('second', 1): ((1, 0),),
    ('third', 0): ((1, 1),),
    ('third', 1): ((2, 0),),
    ('fourth', 0): ((2, 1),),
    ('fourth', 1): ((3, 0),),
    ('hidden', 0): ((3, 1),),
    ('hidden', 1): ((4, 0),),
    ('gather', 0): ((4, 1),),
    ('pass', 1): ((5, 0),),
    ('pass', 5): ((5, 1),),
    ('pass', 9): ((6, 0),),
    ('last', 0): ((6, 1),),
}
DP = ("y", "xl", "c")
MP = ("z", "xh")
F = 640
CHUNKS = ((0, 256), (256, 384))
MESH = pl.DeviceIdType.MESH
BF = jnp.bfloat16
F32 = jnp.float32


def dot(a, b):
    return jnp.dot(a, b, preferred_element_type=F32)


def block_kernel(
    tok_in, gw_in, uw_in, wd_in, out,
    tok, w_a, tok_b, w_b, part, xs, xr, down, acc, got, ring_bufs,
    in_s, ex_s, ex_r, r1_s, r1_r, r2_s, r2_r, r3_s, r3_r, r4_s, r4_r, x_s, x_r,
    za_s, za_r, ya_s, ya_r, xa_s, xa_r, cf_s, cf_r, zr_s, zr_r, xh_s, xh_r,
):
    y, xl, c, z, xh = (lax.axis_index(a) for a in AXES)
    other_x, other_c = 1 - xl, 1 - c

    def at_y(d):
        return lax.rem(y + (d + NY), NY)

    def at_z(d):
        return lax.rem(z + (d + NZ), NZ)

    def put(src, dst, ss, rs, **where):
        return pltpu.make_async_remote_copy(
            src_ref=src, dst_ref=dst, send_sem=ss, recv_sem=rs,
            device_id=where, device_id_type=MESH,
        )

    barrier = pltpu.get_barrier_semaphore()

    def greet(**where):
        pl.semaphore_signal(barrier, inc=1, device_id=where, device_id_type=MESH)

    greet(c=other_c)
    greet(xl=other_x)
    greet(xh=1 - xh)
    for d in range(1, NY):
        greet(y=at_y(d))
    for d in (1, -1):
        greet(y=at_y(d), xl=other_x)
        greet(z=at_z(d))
    group = z // 3
    active = c == lax.rem(group, 2)
    for k in range(6):

        @pl.when(active & (z != 6 * xl + k))
        def _():
            greet(xl=group // 2, z=6 * xl + k)

    loads = [
        pltpu.make_async_copy(src, dst, in_s.at[k])
        for k, (src, dst) in enumerate(
            ((gw_in, w_a.at[0]), (uw_in, w_a.at[1]), (tok_in, tok), (wd_in, down.at[z]))
        )
    ]
    for cp in loads:
        cp.start()
    for cp in loads:
        cp.wait()
    my_first = 6 * xl + 3 * c
    mine = (z >= my_first) & (z < my_first + 3)
    pl.semaphore_wait(barrier, 3 + (NY - 1) + 4 + 3 - mine.astype(jnp.int32))

    def ring(i, h, k):
        sign = (1, -1)[i]
        block = down.at[at_z(-sign * (k - 1)), pl.ds(320 * h, 320)]
        return put(block, block, zr_s.at[i, h, k], zr_r.at[i, h, k], z=at_z(sign))

    def last(i, h):
        return 6 if i == h else 5

    def advance(k, h):
        for i in range(2):
            if k <= last(i, h):
                sign = (1, -1)[i]
                block = down.at[at_z(-sign * k), pl.ds(320 * h, 320)]
                put(block, block, zr_s.at[i, h, k], zr_r.at[i, h, k], z=at_z(sign)).wait_recv()
            if k < last(i, h):
                ring(i, h, k + 1).start()

    def onward(stage, n):
        for k, h in WHEN.get((stage, n), ()):
            advance(k, h)

    exchange = [
        put(tok.at[pl.ds(6 * h + 3 * other_c, 3)], tok_b.at[h], ex_s.at[h], ex_r.at[h], c=other_c)
        for h in range(2)
    ] + [
        put(w_a.at[k], w_b.at[k], ex_s.at[2 + k], ex_r.at[2 + k], c=other_c)
        for k in range(2)
    ]
    for cp in exchange:
        cp.start()
    for h in range(2):
        for i in range(2):
            ring(i, h, 1).start()
    for k in range(2):
        for h in range(2):
            a = tok[pl.ds(6 * h + 3 * c, 3)].reshape(384, 256)
            part[k, h] = dot(a, w_a[k]).reshape(3, NY, 16, F)
    for cp in exchange:
        cp.wait_recv()

    sent = list(exchange)

    def go(cp):
        cp.start()
        sent.append(cp)
        return cp

    def own(k, h, o):
        return part[k, h, :, o].reshape(48, F)

    def cols(n):
        return pl.ds(CHUNKS[n][0], CHUNKS[n][1])

    def own_cols(k, h, o, n):
        return part[k, h, :, o, :, cols(n)].reshape(48, CHUNKS[n][1])

    def bufs(n):
        return ring_bufs[n]

    def long_way(n):
        return n % 2

    step1, step2, step3, step4 = {}, {}, {}, {}
    many = range(len(CHUNKS))
    far = at_y(4)
    for n in many:
        s1s, s1r = bufs(n)[0:2]
        for k in range(2):
            for h in range(2):
                a = tok_b[h, :, far].reshape(48, 256)
                s1s[h, k] = (own_cols(k, h, far, n) + dot(a, w_b[k, :, cols(n)])).astype(BF)
        step1[n] = go(
            put(s1s, s1r, r1_s.at[n], r1_r.at[n], y=at_y((-1, 1)[long_way(n)]))
        )
    for k in range(2):
        for h in range(2):
            a = tok_b[h].reshape(384, 256)
            part[k, h] = part[k, h] + dot(a, w_b[k]).reshape(3, NY, 16, F)

    def second(n, i):
        s1r, s2s, s2r = bufs(n)[1:4]
        sign = (-1, 1)[i]
        for k in range(2):
            for h in range(2):
                v = own_cols(k, h, at_y(3 * sign), n)
                if i == long_way(n):
                    v = v + s1r[h, k].astype(F32)
                s2s[i, h, k] = v.astype(BF)
        step2[n, i] = go(
            put(s2s.at[i], s2r.at[i], r2_s.at[n, i], r2_r.at[n, i], y=at_y(sign))
        )

    for n in many:
        second(n, 1 - long_way(n))
    crossing = []
    for j in range(3):
        for k in range(2):
            xs[j, k] = own(k, other_x, at_y(j - 1)).astype(BF)
        crossing.append(go(put(xs.at[j], xr.at[j], x_s.at[j], x_r.at[j], xl=other_x)))
    for n in many:
        step1[n].wait_recv()
        second(n, long_way(n))
        onward('second', n)

    def third(n, i):
        s2r, s3s, s3r = bufs(n)[3:6]
        sign = (-1, 1)[i]
        step2[n, i].wait_recv()
        for k in range(2):
            for h in range(2):
                s3s[i, h, k] = (
                    own_cols(k, h, at_y(2 * sign), n) + s2r[i, h, k].astype(F32)
                ).astype(BF)
        for t, where in ((0, xl), (1, other_x)):
            step3[n, i, t] = go(
                put(
                    s3s.at[i, where], s3r.at[i, t], r3_s.at[n, i, t], r3_r.at[n, i, t],
                    y=at_y(sign), xl=where,
                )
            )

    for n in many:
        third(n, 1 - long_way(n))
        third(n, long_way(n))
        onward('third', n)

    crossing[0].wait_recv()
    crossing[2].wait_recv()

    def fourth(n, i):
        s3r, s4s, s4r = bufs(n)[5:8]
        sign = (-1, 1)[i]
        for t in range(2):
            step3[n, i, t].wait_recv()
        for k in range(2):
            s4s[i, k] = (
                own_cols(k, xl, at_y(sign), n)
                + s3r[i, 0, k].astype(F32)
                + s3r[i, 1, k].astype(F32)
                + xr[1 + sign, k, :, cols(n)].astype(F32)
            )
        step4[n, i] = go(
            put(s4s.at[i], s4r.at[i], r4_s.at[n, i], r4_r.at[n, i], y=at_y(sign))
        )

    for n in many:
        fourth(n, 1 - long_way(n))
        fourth(n, long_way(n))
        onward('fourth', n)
    crossing[1].wait_recv()

    to_x = z // 6
    row = pl.multiple_of(16 * y, 16)

    def slot(n):
        w = CHUNKS[n][1]
        return bufs(n)[9].at[pl.ds(row, 16), pl.ds(pl.multiple_of(z * w, 128), w)]

    def along_z(n, j):
        return put(
            bufs(n)[8].at[j], slot(n), za_s.at[n, j], za_r.at[n], z=my_first + j, xl=to_x
        )

    for n in many:
        s4r, hid = bufs(n)[7:9]
        for i in range(2):
            step4[n, i].wait_recv()
        gate, up = (
            own_cols(k, xl, y, n) + s4r[0, k] + s4r[1, k] + xr[1, k, :, cols(n)].astype(F32)
            for k in range(2)
        )
        hid[...] = (jax.nn.silu(gate) * up).astype(BF).reshape(hid.shape)
        for j in range(3):

            @pl.when(my_first + j != z)
            def _():
                along_z(n, j).start()

            @pl.when(my_first + j == z)
            def _():
                pltpu.make_async_copy(hid.at[j], slot(n), za_r.at[n]).start()

        onward('hidden', n)


    order = (1, 7, 2, 6, 3, 5, 4)

    def piece(n, d, x):
        start = pl.multiple_of(16 * at_y(-d), 16)
        w = 6 * CHUNKS[n][1]
        return bufs(n)[9].at[pl.ds(start, 16), pl.ds(pl.multiple_of(w * x, 128), w)]

    def along_y(n, d):
        p = piece(n, 0, xl)
        return put(p, p, ya_s.at[n, d], ya_r.at[n, d], y=at_y(d))

    def across(n, d):
        p = piece(n, d, xl)
        return put(p, p, xa_s.at[n, d], xa_r.at[n, d], xl=other_x)

    def to_core(n, d, t):
        p = piece(n, d, xl if t == 0 else other_x)
        return put(p, p, cf_s.at[n, t, d], cf_r.at[n, t, d], c=other_c)

    for n in many:

        @pl.when(active)
        def _():
            p = piece(n, 0, xl)
            pltpu.make_async_copy(p, p, za_r.at[n]).wait()
            for d in order[:-1]:
                along_y(n, d).start()
            across(n, 0).start()
            to_core(n, 0, 0).start()

        onward('gather', n)

    def passed_on(n):
        d, sign = ((3, 1), (5, -1))[n % 2]
        p = piece(n, d, xl)
        return put(p, p, ya_s.at[n, 4], ya_r.at[n, 4], y=at_y(sign))

    def came_along(n, d):
        p = piece(n, d, xl)
        put(p, p, ya_s.at[n, d], ya_r.at[n, d], y=at_y(d)).wait_recv()
        if d == (3, 5)[n % 2]:
            passed_on(n).start()
        across(n, d).start()
        to_core(n, d, 0).start()

    def came_across(n, d):
        p = piece(n, d, other_x)
        put(p, p, xa_s.at[n, d], xa_r.at[n, d], xl=other_x).wait_recv()
        to_core(n, d, 1).start()

    events = [(n, d) for n in many for d in order]
    crossed = [(n, d) for n in many for d in (0, *order)]

    def order_of(d):
        return (0, *order).index(d) - 1

    @pl.when(active)
    def _():
        done = 0
        for count, (n, d) in enumerate(events):
            came_along(n, d)
            while done < len(crossed) and crossed[done][0] * 7 + order_of(crossed[done][1]) + 4 < count:
                came_across(*crossed[done])
                done += 1
            onward('pass', count)
        for at in crossed[done:]:
            came_across(*at)

    @pl.when(jnp.logical_not(active))
    def _():
        for count, (n, d) in enumerate(crossed):
            for t in range(2):
                to_core(n, d, t).wait_recv()
            onward('pass', count)

    onward('last', 0)

    def rows_of(t):
        r = pl.ds(pl.multiple_of(64 * t, 64), 64)
        return sum(
            dot(bufs(n)[9][r, :], down[:, cols(n), :].reshape(NZ * CHUNKS[n][1], 256))
            for n in many
        )

    acc[...] = rows_of(1 - xh)
    final = put(acc, got, xh_s, xh_r, xh=1 - xh)
    final.start()
    result = rows_of(xh)
    final.wait_recv()
    out[...] = (result + got[...]).astype(BF)

    final.wait_send()
    for n in many:
        for j in range(3):

            @pl.when(my_first + j != z)
            def _():
                along_z(n, j).wait_send()

    @pl.when(active)
    def _():
        for n in many:
            for d in order[:-1]:
                along_y(n, d).wait_send()
            passed_on(n).wait_send()
            for d in (0, *order):
                across(n, d).wait_send()
                for t in range(2):
                    to_core(n, d, t).wait_send()

    for h in range(2):
        for i in range(2):
            for k in range(1, last(i, h) + 1):
                ring(i, h, k).wait_send()
    for cp in sent:
        cp.wait_send()


def body(tokens, gate_weight, up_weight, down_weight):
    dma = pltpu.SemaphoreType.DMA
    m = len(CHUNKS)

    def chunk_bufs(w):
        return [
            *[pltpu.VMEM((2, 2, 48, w), BF)] * 2,
            *[pltpu.VMEM((2, 2, 2, 48, w), BF)] * 4,
            *[pltpu.VMEM((2, 2, 48, w), F32)] * 2,
            pltpu.VMEM((3, 16, w), BF),
            pltpu.VMEM((16 * NY, NZ * w), BF),
        ]

    return pl.pallas_call(
        block_kernel,
        out_shape=jax.ShapeDtypeStruct((64, 256), BF),
        in_specs=[pl.BlockSpec(memory_space=pltpu.HBM)] * 4,
        out_specs=pl.BlockSpec(memory_space=pltpu.VMEM),
        scratch_shapes=[
            pltpu.VMEM((NZ, NY, 16, 256), BF),
            pltpu.VMEM((2, 256, F), BF),
            pltpu.VMEM((2, 3, NY, 16, 256), BF),
            pltpu.VMEM((2, 256, F), BF),
            pltpu.VMEM((2, 2, 3, NY, 16, F), F32),
            *[pltpu.VMEM((3, 2, 48, F), BF)] * 2,
            pltpu.VMEM((NZ, F, 256), BF),
            *[pltpu.VMEM((64, 256), F32)] * 2,
            [chunk_bufs(w) for _, w in CHUNKS],
            dma((4,)),
            *[dma((4,))] * 2, *[dma((m,))] * 2, *[dma((m, 2))] * 2,
            *[dma((m, 2, 2))] * 2, *[dma((m, 2))] * 2, *[dma((3,))] * 2,
            dma((m, 3)), dma((m,)), *[dma((m, NY))] * 4, *[dma((m, 2, NY))] * 2,
            *[dma((2, 2, 7))] * 2, dma, dma,
        ],
        compiler_params=pltpu.CompilerParams(
            collective_id=0, has_side_effects=True, vmem_limit_bytes=55040 << 10
        ),
    )(tokens.reshape(NZ, NY, 16, 256), gate_weight, up_weight, down_weight)


def solution(mesh):
    split = Mesh(mesh.devices.reshape(NY, 2, 2, NZ, 2), AXES)
    in_specs = (P(None, DP), P(DP, MP), P(DP, MP), P(MP, DP))
    return jax.shard_map(body, mesh=split, in_specs=in_specs, out_specs=P(MP, DP), check_vma=False)
```
